32 devices in a mesh: expert: 8 (over z, y), pipe: 4 (over x, core).
Axes of the slice: x: 2, y: 2, z: 4, core: 2. Of those that a mesh axis runs over, the one named last changes fastest.
Arguments:
- layer_input: bfloat16 [4, 2048, 7168], P('pipe', 'expert'), may hold values from -6 to 6
- output_grad: bfloat16 [4, 2048, 7168], P('pipe', 'expert'), may hold values from -6 to 6
- gate_weight: bfloat16 [4, 7168, 1024], P('pipe', None, 'expert'), may hold values from -0.0625 to 0.0625
- up_weight: bfloat16 [4, 7168, 1024], P('pipe', None, 'expert'), may hold values from -0.0625 to 0.0625
- down_weight: bfloat16 [4, 1024, 7168], P('pipe', 'expert'), may hold values from -0.1875 to 0.1875
- expert_ids: int32 [4, 2048, 8], P('pipe', 'expert'), may hold values from 0 to 255, as said below
- slots: int32 [4, 2048, 8], P('pipe', 'expert'), may hold values from 0 to 32, as said below
- combine_weights: bfloat16 [4, 2048, 8], P('pipe', 'expert'), may hold values from 0.099609375 to 0.59765625
Outputs:
- prev_grad: bfloat16 [4, 2048, 7168], P('pipe', 'expert')
- gate_grad: bfloat16 [4, 7168, 1024], P('pipe', None, 'expert')
- up_grad: bfloat16 [4, 7168, 1024], P('pipe', None, 'expert')
- down_grad: bfloat16 [4, 1024, 7168], P('pipe', 'expert')
- router_grad: float32 [4, 2048, 8], P('pipe', 'expert')
The draws below stay inside these ranges and needn't reach their ends.
Inputs may be any that keep to these rules, and one draw needn't show every extreme that they name: `expert_ids`: each token names 8 different experts. In every section one expert below 1 is named by more than 32 tokens of every device's 256 tokens. `slots`: A token's slot for an expert counts the earlier tokens of the same device's 256 tokens that name that expert, capped at 32, which marks a dropped token.
All inputs are finite; a program needn't handle non-finite values.
Results may differ from the reference program's by a relative error of at most 0.015.
Values may be sent and summed in bfloat16 or wider, within the bound.
A program may use at most 128 MiB of HBM per device.

```python
import jax
import jax.numpy as jnp
from jax import lax

D = 7168
FF = 1024
EXPERTS = 256
TOPK = 8
GROUP = 8
TOK_DEV = 256
CAP = 32
EXP_WIN = 1
HIDDEN_SIZE = 1024
TOKENS = 2048
SECTIONS = 4
N_EXPERT = 8


def routing_tables(key):
    noise = jax.random.randint(jax.random.fold_in(key, 101), (SECTIONS, TOKENS, EXPERTS), 0, 2 ** 20)
    scores = noise * EXPERTS + jnp.arange(EXPERTS, dtype=jnp.int32)
    favourite = jax.random.randint(jax.random.fold_in(key, 102), (SECTIONS, 1, 1), 0, EXP_WIN)
    blocks = TOKENS // TOK_DEV
    order_noise = jax.random.randint(jax.random.fold_in(key, 103), (SECTIONS, blocks, TOK_DEV), 0, 2 ** 16)
    distinct = order_noise * TOK_DEV + jnp.arange(TOK_DEV, dtype=jnp.int32)
    ranking = jnp.argsort(jnp.argsort(distinct, axis=-1), axis=-1).astype(jnp.int32).reshape(SECTIONS, TOKENS, 1)
    chosen = (ranking < CAP + CAP // 2) & (jnp.arange(EXPERTS, dtype=jnp.int32)[None, None, :] == favourite)
    scores = scores + chosen.astype(jnp.int32) * 2 ** 29
    picked = lax.top_k(scores, TOPK)[1].astype(jnp.int32)
    counting = jnp.zeros((SECTIONS, TOKENS, EXPERTS), jnp.int32)
    for column in range(TOPK):
        counting = counting + (picked[:, :, column:column + 1] == jnp.arange(EXPERTS, dtype=jnp.int32)[None, None, :]).astype(jnp.int32)
    counting = counting.reshape(SECTIONS, blocks, TOK_DEV, EXPERTS)
    earlier = (jnp.cumsum(counting, axis=2) - counting).reshape(SECTIONS, TOKENS, EXPERTS)
    placed = jnp.take_along_axis(earlier, picked, axis=2)
    return (picked, jnp.minimum(placed, CAP).astype(jnp.int32))


def draw_expert_ids(key, part):
    return routing_tables(key)[0]


def draw_slots(key, part):
    return routing_tables(key)[1]


def block_scale(rng, dims, pieces, least, high):
    gain = 1.0
    for axis_at, parts in pieces:
        heights = jax.random.uniform(jax.random.fold_in(jax.random.fold_in(rng, 6), axis_at), (parts,), jnp.float32, least / len(pieces), high / len(pieces))
        gain = gain * jnp.repeat(jnp.exp(heights), dims[axis_at] // parts).reshape((-1,) + (1,) * (len(dims) - 1 - axis_at))
    return gain


def gaussian(own_key, extent, width, most, cuts=(), kind=jnp.bfloat16):
    array = jax.random.normal(own_key, extent, jnp.float32) * width
    if len(cuts) > 0:
        array = block_scale(own_key, extent, cuts, -0.22, 0.18) * array
    return jnp.clip(array, min=-most, max=most).astype(kind)


def setup_inputs(seed: int = 0) -> dict:
    streams_of = jax.random.split(jax.random.key(seed), 9)
    layer_input = gaussian(streams_of[0], (SECTIONS, TOKENS, D), 1.0, 6.0, ((0, 4), (1, 8)))
    output_grad = gaussian(streams_of[1], (SECTIONS, TOKENS, D), 1.0, 6.0, ((0, 4), (1, 8)))
    gate_weight = gaussian(streams_of[2], (SECTIONS, D, HIDDEN_SIZE), D ** -0.5, 0.0625, ((0, 4), (2, 8)))
    up_weight = gaussian(streams_of[3], (SECTIONS, D, HIDDEN_SIZE), D ** -0.5, 0.0625, ((0, 4), (2, 8)))
    down_weight = gaussian(streams_of[4], (SECTIONS, HIDDEN_SIZE, D), FF ** -0.5, 0.1875, ((0, 4), (1, 8)))
    expert_ids = draw_expert_ids(jax.random.fold_in(streams_of[8], 71), 0)
    slots = draw_slots(jax.random.fold_in(streams_of[8], 71), 0)
    combine_weights = jnp.clip(0.099609375 + 0.49804688 * jax.random.uniform(streams_of[7], (SECTIONS, TOKENS, TOPK), jnp.float32) ** block_scale(streams_of[7], (SECTIONS, TOKENS, TOPK), ((0, 4), (1, 8)), -0.2, 0.2), 0.099609375, 0.59765625).astype(jnp.bfloat16)
    return {"layer_input": layer_input, "output_grad": output_grad, "gate_weight": gate_weight, "up_weight": up_weight, "down_weight": down_weight, "expert_ids": expert_ids, "slots": slots, "combine_weights": combine_weights}


def rounded(value):
    return lax.optimization_barrier(value.astype(jnp.bfloat16)).astype(jnp.float32)


def section_backward(inputs, upstream, w_gate, w_up, w_down, routes, places, weights):
    blocks = jnp.arange(TOKENS, dtype=jnp.int32) // TOK_DEV
    rows_total = N_EXPERT * CAP
    member = FF // GROUP
    contribution = jnp.zeros((TOKENS, D), jnp.float32)
    router_grad = jnp.zeros((TOKENS, TOPK), jnp.float32)
    gate_list, up_list, down_list = [], [], []
    for expert in range(EXP_WIN):
        token_buffer = jnp.zeros((rows_total, D), jnp.bfloat16)
        grad_buffer = jnp.zeros((rows_total, D), jnp.bfloat16)
        weight_buffer = jnp.zeros((rows_total,), jnp.bfloat16)
        targets = []
        for column in range(TOPK):
            hit = (routes[:, column] == expert) & (places[:, column] < CAP)
            target = jnp.where(hit, blocks * CAP + places[:, column], rows_total).astype(jnp.int32)
            token_buffer = token_buffer.at[target].set(inputs, mode="drop")
            grad_buffer = grad_buffer.at[target].set(upstream, mode="drop")
            weight_buffer = weight_buffer.at[target].set(weights[:, column], mode="drop")
            targets.append((hit, target))
        lower = expert * FF
        gate_cols = w_gate[:, lower:lower + FF]
        up_cols = w_up[:, lower:lower + FF]
        down_rows = w_down[lower:lower + FF, :]
        gate_pre = jnp.dot(token_buffer, gate_cols, preferred_element_type=jnp.float32)
        up_pre = jnp.dot(token_buffer, up_cols, preferred_element_type=jnp.float32)
        sigmoid_gate = jax.nn.sigmoid(gate_pre)
        silu_gate = gate_pre * sigmoid_gate
        hidden = (silu_gate * up_pre).astype(jnp.bfloat16)
        scaled = (weight_buffer.astype(jnp.float32)[:, None] * grad_buffer.astype(jnp.float32)).astype(jnp.bfloat16)
        hidden_split = hidden.astype(jnp.float32).reshape(rows_total, GROUP, member)
        down_split = down_rows.astype(jnp.float32).reshape(GROUP, member, D)
        partial_out = jnp.einsum("rgf,gfd->grd", hidden_split, down_split)
        score_parts = jnp.sum(partial_out * grad_buffer.astype(jnp.float32)[None], axis=2)
        score_sum = jnp.sum(rounded(score_parts), axis=0)
        back_hidden = jnp.dot(scaled, down_rows.T, preferred_element_type=jnp.float32)
        dgate = (back_hidden * up_pre * sigmoid_gate * (1.0 + gate_pre * (1.0 - sigmoid_gate))).astype(jnp.bfloat16)
        dup = (back_hidden * silu_gate).astype(jnp.bfloat16)
        down_list.append(jnp.dot(hidden.T, scaled, preferred_element_type=jnp.float32).astype(jnp.bfloat16))
        gate_list.append(jnp.dot(token_buffer.T, dgate, preferred_element_type=jnp.float32).astype(jnp.bfloat16))
        up_list.append(jnp.dot(token_buffer.T, dup, preferred_element_type=jnp.float32).astype(jnp.bfloat16))
        back_parts = jnp.einsum("rgf,dgf->grd", dgate.astype(jnp.float32).reshape(rows_total, GROUP, member), gate_cols.astype(jnp.float32).reshape(D, GROUP, member))
        back_parts = back_parts + jnp.einsum("rgf,dgf->grd", dup.astype(jnp.float32).reshape(rows_total, GROUP, member), up_cols.astype(jnp.float32).reshape(D, GROUP, member))
        back_sum = jnp.sum(rounded(back_parts), axis=0)
        for column in range(TOPK):
            hit, target = targets[column]
            safe = jnp.minimum(target, rows_total - 1).astype(jnp.int32)
            contribution = contribution + jnp.where(hit[:, None], back_sum[safe], 0.0)
            router_grad = router_grad.at[:, column].add(jnp.where(hit, score_sum[safe], 0.0))
    input_grad = (upstream.astype(jnp.float32) + contribution).astype(jnp.bfloat16)
    gate_grad = jnp.concatenate(gate_list, axis=1)
    up_grad = jnp.concatenate(up_list, axis=1)
    down_grad = jnp.concatenate(down_list, axis=0)
    return input_grad, gate_grad, up_grad, down_grad, router_grad


def reference(layer_input, output_grad, gate_weight, up_weight, down_weight, expert_ids, slots, combine_weights):
    inputs_list, gate_list, up_list, down_list, router_list = [], [], [], [], []
    for section in range(SECTIONS):
        results = section_backward(layer_input[section], output_grad[section], gate_weight[section], up_weight[section], down_weight[section], expert_ids[section], slots[section], combine_weights[section])
        inputs_list.append(results[0])
        gate_list.append(results[1])
        up_list.append(results[2])
        down_list.append(results[3])
        router_list.append(results[4])
    shifted = inputs_list[1:] + [jnp.zeros((TOKENS, D), jnp.bfloat16)]
    return (jnp.stack(shifted), jnp.stack(gate_list), jnp.stack(up_list), jnp.stack(down_list), jnp.stack(router_list))
```

```python
import functools

import jax
import jax.numpy as jnp
from jax import lax
from jax.experimental import pallas as pl
from jax.experimental.pallas import tpu as pltpu
from jax.sharding import PartitionSpec as P

GROUP = 8
CAP = 32
COLS = 2
MESH = pl.DeviceIdType.MESH


def from_behind(x, axis, by):
    size = lax.axis_size(axis)
    pairs = [(i, i + by) for i in range(size) if 0 <= i + by < size]
    return lax.ppermute(x, axis, pairs)


def shards(
    layer_input,
    output_grad,
    gate_weight,
    up_weight,
    down_weight,
    expert_ids,
    slots,
    combine_weights,
):
    devices = lax.axis_size("expert")
    window = devices // GROUP
    width = layer_input.shape[2]
    inputs = layer_input[0]
    upstream_grad = output_grad[0]
    w_gate = gate_weight[0]
    w_up = up_weight[0]
    w_down = down_weight[0]
    routes = expert_ids[0]
    places = slots[0]
    positions = routes * CAP + places
    usable = (routes < window) & (places < CAP)
    columns = lax.broadcasted_iota(jnp.int32, (1, 1, window * CAP), 2)
    picker = ((positions[:, :, None] == columns) & usable[:, :, None]).astype(jnp.float32)
    selection = jnp.sum(picker, axis=1)
    select_half = selection.astype(jnp.bfloat16)
    contract_first = (((0,), (0,)), ((), ()))
    contract_last = (((1,), (1,)), ((), ()))
    token_buffer = lax.dot_general(
        select_half, inputs, contract_first, preferred_element_type=jnp.float32
    ).astype(jnp.bfloat16)
    grad_buffer = lax.dot_general(
        select_half, upstream_grad, contract_first, preferred_element_type=jnp.float32
    ).astype(jnp.bfloat16)
    weight_buffer = jnp.einsum("tkp,tk->p", picker, combine_weights[0].astype(jnp.float32)).astype(
        jnp.bfloat16
    )
    token_blocks = token_buffer.reshape(window, CAP, width)
    grad_blocks = grad_buffer.reshape(window, CAP, width)
    weight_blocks = weight_buffer.reshape(window, CAP)
    collected = (
        lax.all_gather(token_blocks, "expert", axis=0, tiled=True),
        lax.all_gather(grad_blocks, "expert", axis=0, tiled=True),
        lax.all_gather(weight_blocks, "expert", axis=0, tiled=True),
    )
    owner = lax.axis_index("expert") // GROUP
    expert_rows = lax.dynamic_index_in_dim(
        collected[0].reshape(devices, window, CAP, width), owner, 1, False
    )
    expert_grads = lax.dynamic_index_in_dim(
        collected[1].reshape(devices, window, CAP, width), owner, 1, False
    )
    expert_weights = lax.dynamic_index_in_dim(
        collected[2].reshape(devices, window, CAP), owner, 1, False
    )
    flat_rows = expert_rows.reshape(devices * CAP, width)
    flat_grads = expert_grads.reshape(devices * CAP, width)
    flat_weights = expert_weights.reshape(devices * CAP, 1)
    gate_pre = jnp.dot(flat_rows, w_gate, preferred_element_type=jnp.float32)
    up_pre = jnp.dot(flat_rows, w_up, preferred_element_type=jnp.float32)
    sigmoid_gate = jax.nn.sigmoid(gate_pre)
    silu_gate = gate_pre * sigmoid_gate
    hidden = (silu_gate * up_pre).astype(jnp.bfloat16)
    scaled = (flat_weights.astype(jnp.float32) * flat_grads.astype(jnp.float32)).astype(
        jnp.bfloat16
    )
    partial_out = jnp.dot(hidden, w_down, preferred_element_type=jnp.float32)
    score_part = jnp.sum(partial_out * flat_grads.astype(jnp.float32), axis=1)
    back_hidden = lax.dot_general(scaled, w_down, contract_last, preferred_element_type=jnp.float32)
    dgate = (back_hidden * up_pre * sigmoid_gate * (1.0 + gate_pre * (1.0 - sigmoid_gate))).astype(
        jnp.bfloat16
    )
    dup = (back_hidden * silu_gate).astype(jnp.bfloat16)
    down_grad = lax.dot_general(
        hidden, scaled, contract_first, preferred_element_type=jnp.float32
    ).astype(jnp.bfloat16)
    gate_grad = lax.dot_general(
        flat_rows, dgate, contract_first, preferred_element_type=jnp.float32
    ).astype(jnp.bfloat16)
    up_grad = lax.dot_general(
        flat_rows, dup, contract_first, preferred_element_type=jnp.float32
    ).astype(jnp.bfloat16)
    back_input = lax.dot_general(dgate, w_gate, contract_last, preferred_element_type=jnp.float32)
    back_input = back_input + lax.dot_general(
        dup, w_up, contract_last, preferred_element_type=jnp.float32
    )
    back_half = back_input.astype(jnp.bfloat16)
    owner = lax.axis_index("expert") // GROUP
    placing = (lax.broadcasted_iota(jnp.int32, (1, window, 1), 1) == owner).astype(jnp.float32)
    back_terms = (
        back_half.reshape(devices, 1, CAP, width) * placing.astype(jnp.bfloat16)[:, :, :, None]
    )
    score_terms = score_part.reshape(devices, 1, CAP) * placing
    summed, score_summed = (
        lax.psum_scatter(back_terms, "expert", scatter_dimension=0, tiled=True).astype(jnp.float32),
        lax.psum_scatter(
            score_terms.astype(jnp.bfloat16), "expert", scatter_dimension=0, tiled=True
        ).astype(jnp.float32),
    )
    grouped = summed.reshape(window * CAP, width)
    score_sum = score_summed.reshape(window * CAP)
    contribution = jnp.dot(selection, grouped, precision=lax.Precision.HIGHEST)
    input_grad = (upstream_grad.astype(jnp.float32) + contribution).astype(jnp.bfloat16)
    router_grad = jnp.einsum("tkp,p->tk", picker, score_sum, precision=lax.Precision.HIGHEST)
    previous = from_behind(input_grad[None], "pipe", -1)
    return (previous, gate_grad[None], up_grad[None], down_grad[None], router_grad[None])


def cuts(width, count):
    narrow = width // 7 // 128 * 128
    wide = (width - narrow) // count // 128 * 128
    pieces = [(i * wide, wide, True) for i in range(count)]
    return pieces, (count * wide, width - count * wide, False)


def exchange(
    pipes,
    wide_count,
    layer_ref,
    upstream_ref,
    gate_ref,
    up_ref,
    down_ref,
    select_ref,
    weight_ref,
    rows_out,
    grads_out,
    pair_out,
    hidden_out,
    behind_out,
    select_out,
    sums_out,
    score_out,
    layer_buf,
    upstream_buf,
    x_all,
    g_all,
    w_pair,
    w_down,
    part,
    from_y,
    from_above,
    from_below,
    both,
    back,
    temp,
    local_sem,
    ag_rx,
    ag_up,
    ag_dn,
    ag_y,
    rs_y_tx,
    rs_y_rx,
    rs_up_tx,
    rs_up_rx,
    rs_dn_tx,
    rs_dn_rx,
    pipe_tx,
    pipe_rx,
):
    me = lax.axis_index("expert")
    stage = lax.axis_index("pipe")
    y = lax.rem(me, COLS)
    z = lax.div(me, COLS)
    top = GROUP // COLS - 1
    other = 1 - y
    partner = me + 1 - 2 * y
    above, below = me + COLS, me - COLS
    width = layer_ref.shape[1]
    total = x_all.shape[0]
    wide, narrow = cuts(width, wide_count)
    pieces = [narrow] + wide
    count = len(pieces)
    not_top, not_low = z < top, z > 0
    to_pipe, from_pipe = stage > 0, stage < pipes - 1

    def rows(block):
        return pl.ds(pl.multiple_of(block * CAP, CAP), CAP)

    local = []

    def load(src, dst):
        copy = pltpu.make_async_copy(src, dst, local_sem.at[len(local)])
        local.append(copy)
        copy.start()
        return copy

    layer_loads = [
        load(layer_ref.at[:, pl.ds(c, w)], layer_buf.at[:, pl.ds(c, w)]) for c, w, _ in pieces
    ]
    upstream_loads = [
        load(upstream_ref.at[:, pl.ds(c, w)], upstream_buf.at[:, pl.ds(c, w)]) for c, w, _ in pieces
    ]
    weight_loads = [
        load(gate_ref, w_pair.at[:, pl.ds(0, 128)]),
        load(up_ref, w_pair.at[:, pl.ds(128, 128)]),
        load(down_ref, w_down),
    ]

    barrier = pltpu.get_barrier_semaphore()
    pl.semaphore_signal(barrier, inc=1, device_id={"expert": partner}, device_id_type=MESH)

    @pl.when(not_top)
    def _():
        pl.semaphore_signal(barrier, inc=1, device_id={"expert": above}, device_id_type=MESH)

    @pl.when(not_low)
    def _():
        pl.semaphore_signal(barrier, inc=1, device_id={"expert": below}, device_id_type=MESH)

    @pl.when(to_pipe)
    def _():
        pl.semaphore_signal(barrier, inc=1, device_id={"pipe": stage - 1}, device_id_type=MESH)

    @pl.when(from_pipe)
    def _():
        pl.semaphore_signal(barrier, inc=1, device_id={"pipe": stage + 1}, device_id_type=MESH)

    def one(flag):
        return jnp.where(flag, 1, 0).astype(jnp.int32)

    pl.semaphore_wait(barrier, 1 + one(not_top) + one(not_low) + one(to_pipe) + one(from_pipe))

    sent = []

    def send(conds, src, dst, tx, rx, device):
        def make():
            return pltpu.make_async_remote_copy(
                src_ref=src(),
                dst_ref=dst(),
                send_sem=tx(),
                recv_sem=rx(),
                device_id=device,
                device_id_type=MESH,
            )

        guard(conds, lambda: make().start())
        return conds, make

    def guard(conds, run):
        if conds:
            flag = conds[0]
            for cond in conds[1:]:
                flag = flag & cond
            pl.when(flag)(run)
        else:
            run()

    def arrived(ref, tx, rx):
        pltpu.make_async_remote_copy(
            src_ref=ref,
            dst_ref=ref,
            send_sem=tx,
            recv_sem=rx,
            device_id={"expert": partner},
            device_id_type=MESH,
        ).wait_recv()

    messages = []
    for array in (x_all, g_all):
        for c, w, is_wide in pieces:
            if array is g_all and not is_wide:
                w = w + 128
            messages.append((array, c, w, is_wide, len(messages)))

    def gather_send(message, block, conds, tx, device):
        array, c, w, _, n = message
        view = lambda: array.at[rows(block), pl.ds(c, w)]
        return send(
            conds, view, view, lambda: tx.at[block, n], lambda: ag_rx.at[block, n], device
        )

    def gather_wait(message, block):
        array, c, w, _, n = message
        arrived(array.at[rows(block), pl.ds(c, w)], ag_y.at[block, n], ag_rx.at[block, n])

    to_above = {"expert": above}
    to_below = {"expert": below}
    to_partner = {"expert": partner}

    picked = select_ref[...]
    g_all[rows(me), pl.ds(width, 128)] = weight_ref[...]
    for message in messages:
        array, c, w, is_wide, n = message
        at = n % count
        loads, source = (
            (layer_loads, layer_buf) if array is x_all else (upstream_loads, upstream_buf)
        )
        span = pieces[at][1]
        loads[at].wait()
        array[rows(me), pl.ds(c, span)] = jnp.dot(
            picked, source[:, pl.ds(c, span)], preferred_element_type=jnp.float32
        ).astype(jnp.bfloat16)
        sent.append(gather_send(message, me, [], ag_y, to_partner))
        sent.append(gather_send(message, me, [not_top], ag_up, to_above))
        sent.append(gather_send(message, me, [not_low], ag_dn, to_below))

    to_prev = {"pipe": stage - 1}
    sent.append(
        send(
            [to_pipe],
            lambda: select_ref,
            lambda: select_out,
            lambda: pipe_tx.at[0],
            lambda: pipe_rx.at[0],
            to_prev,
        )
    )
    sent.append(
        send(
            [to_pipe],
            lambda: upstream_ref,
            lambda: behind_out,
            lambda: pipe_tx.at[1],
            lambda: pipe_rx.at[1],
            to_prev,
        )
    )

    beside = z * COLS + other
    for message in messages:
        if not message[3]:
            gather_wait(message, beside)
            sent.append(gather_send(message, beside, [not_top], ag_up, to_above))
            sent.append(gather_send(message, beside, [not_low], ag_dn, to_below))

    for k in range(1, top + 1):
        for message in messages:
            for low in (True, False):
                at_z = z - k if low else z + k
                valid = z >= k if low else z + k <= top
                onward, tx, device = (
                    (not_top, ag_up, to_above) if low else (not_low, ag_dn, to_below)
                )
                for column in [y] if message[3] else [y, other]:
                    block = at_z * COLS + column
                    guard([valid], functools.partial(gather_wait, message, block))
                    sent.append(gather_send(message, block, [valid, onward], tx, device))
                    if message[3]:
                        sent.append(gather_send(message, block, [valid], ag_y, to_partner))
    for message in messages:
        if message[3]:
            for at_z in range(top + 1):
                gather_wait(message, at_z * COLS + other)

    for copy in weight_loads:
        copy.wait()
    rows_copy = load(x_all, rows_out)
    grads_copy = load(g_all.at[:, pl.ds(0, width)], grads_out)
    step = width // 7
    both[...] = jnp.zeros_like(both)
    back[...] = jnp.zeros_like(back)

    def forward(i, _):
        at = pl.ds(pl.multiple_of(i * step, 128), step)
        both[...] += jnp.dot(x_all[:, at], w_pair[at, :], preferred_element_type=jnp.float32)
        back[...] += lax.dot_general(
            g_all[:, at],
            w_down[:, at],
            (((1,), (1,)), ((), ())),
            preferred_element_type=jnp.float32,
        )
        return 0

    lax.fori_loop(0, 7, forward, 0)
    gate = both[:, pl.ds(0, 128)]
    up = both[:, pl.ds(128, 128)]
    raw = back[...]
    scale = g_all[:, pl.ds(width, 128)].astype(jnp.float32)
    sigmoid = jax.nn.sigmoid(gate)
    silu = gate * sigmoid
    hidden = (silu * up).astype(jnp.bfloat16).astype(jnp.float32)
    score = jnp.sum(hidden * raw, axis=1, keepdims=True)
    part[:, pl.ds(width, 128)] = jnp.broadcast_to(score, (total, 128)).astype(jnp.bfloat16)
    scaled = scale * raw
    pair_out[:, pl.ds(0, 128)] = (
        scaled * up * sigmoid * (1.0 + gate * (1.0 - sigmoid))
    ).astype(jnp.bfloat16)
    pair_out[:, pl.ds(128, 128)] = (scaled * silu).astype(jnp.bfloat16)
    hidden_out[...] = (hidden * scale).astype(jnp.bfloat16)

    def part_view(buffer, block, n):
        c, w, is_wide = pieces[n]
        return buffer.at[rows(block), pl.ds(c, w if is_wide else w + 128)]

    def part_send(n, block, conds, buffer, tx, rx, device):
        return send(
            conds,
            lambda: part_view(part, block, n),
            lambda: part_view(buffer, block, n),
            lambda: tx.at[block, n],
            lambda: rx.at[block, n],
            device,
        )

    def part_wait(n, block, buffer, tx, rx):
        arrived(part_view(buffer, block, n), tx.at[block, n], rx.at[block, n])

    def order(run):
        for k in range(top, 0, -1):
            run(z - k, z >= k)
            run(z + k, z + k <= top)
        run(z, None)

    for n, (c, w, is_wide) in enumerate(pieces):
        for start in range(c, c + w, 1024):
            at = pl.ds(start, min(1024, c + w - start))
            part[:, at] = lax.dot_general(
                pair_out[...],
                w_pair[at, :],
                (((1,), (1,)), ((), ())),
                preferred_element_type=jnp.float32,
            ).astype(jnp.bfloat16)
        if is_wide:
            order(
                lambda at_z, valid, n=n: sent.append(
                    part_send(
                        n,
                        at_z * COLS + other,
                        [] if valid is None else [valid],
                        from_y,
                        rs_y_tx,
                        rs_y_rx,
                        to_partner,
                    )
                )
            )

    def merge(n, block, terms):
        c, w, is_wide = pieces[n]
        w = w if is_wide else w + 128
        here = (rows(block), pl.ds(c, w))
        temp[:, pl.ds(0, w)] = part[here].astype(jnp.float32)
        for cond, buffer, tx, rx in terms:

            def add(buffer=buffer, tx=tx, rx=rx):
                part_wait(n, block, buffer, tx, rx)
                temp[:, pl.ds(0, w)] += buffer[here].astype(jnp.float32)

            guard([] if cond is None else [cond], add)
        part[here] = temp[:, pl.ds(0, w)].astype(jnp.bfloat16)

    via_y = (None, from_y, rs_y_tx, rs_y_rx)
    via_above = (not_top, from_above, rs_dn_tx, rs_dn_rx)
    via_below = (not_low, from_below, rs_up_tx, rs_up_rx)
    for k in range(top, 0, -1):
        for n in range(count):
            for low in (True, False):
                at_z = z - k if low else z + k
                valid = z >= k if low else z + k <= top
                is_wide = pieces[n][2]
                for column in [y] if is_wide else [y, other]:
                    block = at_z * COLS + column
                    terms = ([via_y] if is_wide else []) + [via_above if low else via_below]
                    guard([valid], functools.partial(merge, n, block, terms))
                    if low:
                        out = (from_above, rs_dn_tx, rs_dn_rx, to_below)
                    else:
                        out = (from_below, rs_up_tx, rs_up_rx, to_above)
                    sent.append(part_send(n, block, [valid], *out))
    for n in range(count):
        c, w, is_wide = pieces[n]
        if is_wide:
            merge(n, me, [via_y, via_above, via_below])
        else:
            merge(n, beside, [via_above, via_below])
            sent.append(part_send(n, beside, [], from_y, rs_y_tx, rs_y_rx, to_partner))
            merge(n, me, [via_above, via_below, via_y])
        sent.append(
            send(
                [to_pipe],
                lambda c=c, w=w: part.at[rows(me), pl.ds(c, w)],
                lambda c=c, w=w: sums_out.at[:, pl.ds(c, w)],
                lambda n=n: pipe_tx.at[2 + n],
                lambda n=n: pipe_rx.at[2 + n],
                to_prev,
            )
        )
    score_out[...] = part[rows(me), pl.ds(width, 128)].astype(jnp.float32)

    @pl.when(from_pipe)
    def _():
        arrived(select_out, pipe_tx.at[0], pipe_rx.at[0])
        arrived(behind_out, pipe_tx.at[1], pipe_rx.at[1])
        for n, (c, w, _) in enumerate(pieces):
            arrived(sums_out.at[:, pl.ds(c, w)], pipe_tx.at[2 + n], pipe_rx.at[2 + n])

    for conds, make in sent:
        guard(conds, lambda make=make: make().wait_send())
    rows_copy.wait()
    grads_copy.wait()


def finish(
    keep, x, g, pair, hidden, behind, select, sums, prev_out, gate_out, up_out, down_out
):
    first = (((0,), (0,)), ((), ()))
    grads = lax.dot_general(x[...], pair[...], first, preferred_element_type=jnp.float32)
    gate_out[...] = grads[:, :128].astype(jnp.bfloat16)
    up_out[...] = grads[:, 128:].astype(jnp.bfloat16)
    down_out[...] = lax.dot_general(
        hidden[...], g[...], first, preferred_element_type=jnp.float32
    ).astype(jnp.bfloat16)
    moved = lax.dot_general(select[...], sums[...], first, preferred_element_type=jnp.float32)
    prev = behind[...].astype(jnp.float32) + moved
    prev_out[...] = jnp.where(keep[0] > 0, prev, 0.0).astype(jnp.bfloat16)


def fused(
    pipes,
    layer_input,
    output_grad,
    gate_weight,
    up_weight,
    down_weight,
    expert_ids,
    slots,
    combine_weights,
):
    _, tokens, width = layer_input.shape
    half = jnp.bfloat16
    units = gate_weight.shape[2]
    total = GROUP * CAP
    routes, places = expert_ids[0], slots[0]
    usable = (routes < 1) & (places < CAP)
    positions = jnp.where(usable, routes * CAP + places, CAP)
    hits = positions.T[:, None, :] == lax.broadcasted_iota(jnp.int32, (1, CAP, 1), 1)
    select = jnp.sum(hits.astype(jnp.float32), axis=0).astype(half)
    weight = jnp.sum(
        jnp.where(hits, combine_weights[0].astype(jnp.float32).T[:, None, :], 0.0), axis=(0, 2)
    )
    weight = jnp.broadcast_to(weight.astype(half)[:, None], (CAP, 128))
    wide_count = 3
    wide, narrow = cuts(width, wide_count)
    count = len(wide) + 1
    widest = max([w for _, w, _ in wide] + [narrow[1] + 128])
    dma = pltpu.SemaphoreType.DMA
    vmem = pl.BlockSpec(memory_space=pltpu.VMEM)
    hbm = pl.BlockSpec(memory_space=pl.ANY)
    shape = jax.ShapeDtypeStruct
    x_all, g_all, pair, hidden, behind, select_next, sums, score = pl.pallas_call(
        functools.partial(exchange, pipes, wide_count),
        out_shape=(
            shape((total, width), half),
            shape((total, width), half),
            shape((total, 2 * units), half),
            shape((total, units), half),
            shape((tokens, width), half),
            shape((CAP, tokens), half),
            shape((CAP, width), half),
            shape((CAP, 128), jnp.float32),
        ),
        in_specs=[hbm, hbm, hbm, hbm, hbm, vmem, vmem],
        out_specs=(hbm, hbm, vmem, vmem, hbm, hbm, hbm, vmem),
        scratch_shapes=[
            pltpu.VMEM((tokens, width), half),
            pltpu.VMEM((tokens, width), half),
            pltpu.VMEM((total, width), half),
            pltpu.VMEM((total, width + 128), half),
            pltpu.VMEM((width, 2 * units), half),
            pltpu.VMEM((units, width), half),
            pltpu.VMEM((total, width + 128), half),
            pltpu.VMEM((total, width + 128), half),
            pltpu.VMEM((total, width + 128), half),
            pltpu.VMEM((total, width + 128), half),
            pltpu.VMEM((total, 2 * units), jnp.float32),
            pltpu.VMEM((total, units), jnp.float32),
            pltpu.VMEM((CAP, widest), jnp.float32),
            dma((2 * count + 5,)),
            *[dma((GROUP, 2 * count)) for _ in range(4)],
            *[dma((GROUP, count)) for _ in range(6)],
            dma((2 + count,)),
            dma((2 + count,)),
        ],
        compiler_params=pltpu.CompilerParams(
            collective_id=0, has_side_effects=True, vmem_limit_bytes=50 * 1024 * 1024
        ),
        name="exchange",
    )(
        layer_input[0],
        output_grad[0],
        gate_weight[0],
        up_weight[0],
        down_weight[0],
        select,
        weight,
    )
    keep = jnp.where(lax.axis_index("pipe") < pipes - 1, 1, 0).astype(jnp.int32).reshape(1)
    tile = width // 7
    across = lambda height: pl.BlockSpec((height, tile), lambda i: (0, i))
    along = pl.BlockSpec((tile, units), lambda i: (i, 0))
    whole = lambda *dims: pl.BlockSpec(dims, lambda i: (0, 0))
    prev, gate_grad, up_grad, down_grad = pl.pallas_call(
        finish,
        grid=(7,),
        out_shape=(
            shape((tokens, width), half),
            shape((width, units), half),
            shape((width, units), half),
            shape((units, width), half),
        ),
        in_specs=[
            pl.BlockSpec(memory_space=pltpu.SMEM),
            across(total),
            across(total),
            whole(total, 2 * units),
            whole(total, units),
            across(tokens),
            whole(CAP, tokens),
            across(CAP),
        ],
        out_specs=(across(tokens), along, along, across(units)),
        compiler_params=pltpu.CompilerParams(vmem_limit_bytes=40 * 1024 * 1024),
        name="finish",
    )(keep, x_all, g_all, pair, hidden, behind, select_next, sums)
    router_grad = jnp.sum(jnp.where(hits, score[:, 0][None, :, None], 0.0), axis=1).T
    return (prev[None], gate_grad[None], up_grad[None], down_grad[None], router_grad[None])


def solution(mesh):
    body = shards
    if mesh.shape["expert"] == GROUP:
        body = functools.partial(fused, mesh.shape["pipe"])
    return jax.shard_map(
        body,
        mesh=mesh,
        in_specs=(
            P("pipe", "expert", None),
            P("pipe", "expert", None),
            P("pipe", None, "expert"),
            P("pipe", None, "expert"),
            P("pipe", "expert", None),
            P("pipe", "expert", None),
            P("pipe", "expert", None),
            P("pipe", "expert", None),
        ),
        out_specs=(
            P("pipe", "expert", None),
            P("pipe", None, "expert"),
            P("pipe", None, "expert"),
            P("pipe", "expert", None),
            P("pipe", "expert", None),
        ),
        check_vma=False,
    )
```

```python
import functools

import jax
import jax.numpy as jnp
from jax import lax
from jax.experimental import pallas as pl
from jax.experimental.pallas import tpu as pltpu
from jax.sharding import PartitionSpec as P

GROUP = 8
CAP = 32
COLS = 2
HALF = CAP // 2
MESH = pl.DeviceIdType.MESH


def from_behind(x, axis, by):
    size = lax.axis_size(axis)
    pairs = [(i, i + by) for i in range(size) if 0 <= i + by < size]
    return lax.ppermute(x, axis, pairs)


def shards(
    layer_input,
    output_grad,
    gate_weight,
    up_weight,
    down_weight,
    expert_ids,
    slots,
    combine_weights,
):
    devices = lax.axis_size("expert")
    window = devices // GROUP
    width = layer_input.shape[2]
    inputs = layer_input[0]
    upstream_grad = output_grad[0]
    w_gate = gate_weight[0]
    w_up = up_weight[0]
    w_down = down_weight[0]
    routes = expert_ids[0]
    places = slots[0]
    positions = routes * CAP + places
    usable = (routes < window) & (places < CAP)
    columns = lax.broadcasted_iota(jnp.int32, (1, 1, window * CAP), 2)
    picker = ((positions[:, :, None] == columns) & usable[:, :, None]).astype(jnp.float32)
    selection = jnp.sum(picker, axis=1)
    select_half = selection.astype(jnp.bfloat16)
    contract_first = (((0,), (0,)), ((), ()))
    contract_last = (((1,), (1,)), ((), ()))
    token_buffer = lax.dot_general(
        select_half, inputs, contract_first, preferred_element_type=jnp.float32
    ).astype(jnp.bfloat16)
    grad_buffer = lax.dot_general(
        select_half, upstream_grad, contract_first, preferred_element_type=jnp.float32
    ).astype(jnp.bfloat16)
    weight_buffer = jnp.einsum("tkp,tk->p", picker, combine_weights[0].astype(jnp.float32)).astype(
        jnp.bfloat16
    )
    token_blocks = token_buffer.reshape(window, CAP, width)
    grad_blocks = grad_buffer.reshape(window, CAP, width)
    weight_blocks = weight_buffer.reshape(window, CAP)
    collected = (
        lax.all_gather(token_blocks, "expert", axis=0, tiled=True),
        lax.all_gather(grad_blocks, "expert", axis=0, tiled=True),
        lax.all_gather(weight_blocks, "expert", axis=0, tiled=True),
    )
    owner = lax.axis_index("expert") // GROUP
    expert_rows = lax.dynamic_index_in_dim(
        collected[0].reshape(devices, window, CAP, width), owner, 1, False
    )
    expert_grads = lax.dynamic_index_in_dim(
        collected[1].reshape(devices, window, CAP, width), owner, 1, False
    )
    expert_weights = lax.dynamic_index_in_dim(
        collected[2].reshape(devices, window, CAP), owner, 1, False
    )
    flat_rows = expert_rows.reshape(devices * CAP, width)
    flat_grads = expert_grads.reshape(devices * CAP, width)
    flat_weights = expert_weights.reshape(devices * CAP, 1)
    gate_pre = jnp.dot(flat_rows, w_gate, preferred_element_type=jnp.float32)
    up_pre = jnp.dot(flat_rows, w_up, preferred_element_type=jnp.float32)
    sigmoid_gate = jax.nn.sigmoid(gate_pre)
    silu_gate = gate_pre * sigmoid_gate
    hidden = (silu_gate * up_pre).astype(jnp.bfloat16)
    scaled = (flat_weights.astype(jnp.float32) * flat_grads.astype(jnp.float32)).astype(
        jnp.bfloat16
    )
    partial_out = jnp.dot(hidden, w_down, preferred_element_type=jnp.float32)
    score_part = jnp.sum(partial_out * flat_grads.astype(jnp.float32), axis=1)
    back_hidden = lax.dot_general(scaled, w_down, contract_last, preferred_element_type=jnp.float32)
    dgate = (back_hidden * up_pre * sigmoid_gate * (1.0 + gate_pre * (1.0 - sigmoid_gate))).astype(
        jnp.bfloat16
    )
    dup = (back_hidden * silu_gate).astype(jnp.bfloat16)
    down_grad = lax.dot_general(
        hidden, scaled, contract_first, preferred_element_type=jnp.float32
    ).astype(jnp.bfloat16)
    gate_grad = lax.dot_general(
        flat_rows, dgate, contract_first, preferred_element_type=jnp.float32
    ).astype(jnp.bfloat16)
    up_grad = lax.dot_general(
        flat_rows, dup, contract_first, preferred_element_type=jnp.float32
    ).astype(jnp.bfloat16)
    back_input = lax.dot_general(dgate, w_gate, contract_last, preferred_element_type=jnp.float32)
    back_input = back_input + lax.dot_general(
        dup, w_up, contract_last, preferred_element_type=jnp.float32
    )
    back_half = back_input.astype(jnp.bfloat16)
    owner = lax.axis_index("expert") // GROUP
    placing = (lax.broadcasted_iota(jnp.int32, (1, window, 1), 1) == owner).astype(jnp.float32)
    back_terms = (
        back_half.reshape(devices, 1, CAP, width) * placing.astype(jnp.bfloat16)[:, :, :, None]
    )
    score_terms = score_part.reshape(devices, 1, CAP) * placing
    summed, score_summed = (
        lax.psum_scatter(back_terms, "expert", scatter_dimension=0, tiled=True).astype(jnp.float32),
        lax.psum_scatter(
            score_terms.astype(jnp.bfloat16), "expert", scatter_dimension=0, tiled=True
        ).astype(jnp.float32),
    )
    grouped = summed.reshape(window * CAP, width)
    score_sum = score_summed.reshape(window * CAP)
    contribution = jnp.dot(selection, grouped, precision=lax.Precision.HIGHEST)
    input_grad = (upstream_grad.astype(jnp.float32) + contribution).astype(jnp.bfloat16)
    router_grad = jnp.einsum("tkp,p->tk", picker, score_sum, precision=lax.Precision.HIGHEST)
    previous = from_behind(input_grad[None], "pipe", -1)
    return (previous, gate_grad[None], up_grad[None], down_grad[None], router_grad[None])


def cuts(width, shares, narrow_count):
    unit = width // 7 // 128 * 128
    pieces, at = [], 0
    for share in shares:
        pieces.append((at, share * unit, True))
        at += share * unit
    step = (width - at) // narrow_count // 128 * 128
    narrow = []
    for i in range(narrow_count):
        w = step if i < narrow_count - 1 else width - at
        narrow.append((at, w, False))
        at += w
    return narrow + pieces


def plan(width):
    gather = cuts(width, (3, 3), 1)
    return gather, (cuts(width, (2,), 2), cuts(width, (2, 2, 2), 1))


def exchange(
    pipes,
    layer_ref,
    upstream_ref,
    gate_ref,
    up_ref,
    down_ref,
    select_ref,
    weight_ref,
    rows_out,
    grads_out,
    pair_out,
    hidden_out,
    behind_out,
    select_out,
    sums_out,
    score_out,
    layer_buf,
    upstream_buf,
    x_all,
    g_all,
    w_pair,
    w_down,
    part,
    from_y,
    from_above,
    from_below,
    both,
    back,
    temp,
    local_sem,
    ag_rx,
    ag_up,
    ag_dn,
    ag_y,
    rs_y_tx,
    rs_y_rx,
    rs_up_tx,
    rs_up_rx,
    rs_dn_tx,
    rs_dn_rx,
    pipe_tx,
    pipe_rx,
):
    me = lax.axis_index("expert")
    stage = lax.axis_index("pipe")
    y = lax.rem(me, COLS)
    z = lax.div(me, COLS)
    top = GROUP // COLS - 1
    other = 1 - y
    partner = me + 1 - 2 * y
    above, below = me + COLS, me - COLS
    width = layer_ref.shape[1]
    total = x_all.shape[0]
    pieces, sum_pieces = plan(width)
    count = len(pieces)
    span = total // 2
    not_top, not_low = z < top, z > 0
    to_pipe, from_pipe = stage > 0, stage < pipes - 1

    def rows(half, block):
        return pl.ds(pl.multiple_of(half * span + block * HALF, HALF), HALF)

    local = []

    def load(src, dst):
        copy = pltpu.make_async_copy(src, dst, local_sem.at[len(local)])
        local.append(copy)
        copy.start()
        return copy

    layer_loads = [
        load(layer_ref.at[:, pl.ds(c, w)], layer_buf.at[:, pl.ds(c, w)]) for c, w, _ in pieces
    ]
    upstream_loads = [
        load(upstream_ref.at[:, pl.ds(c, w)], upstream_buf.at[:, pl.ds(c, w)]) for c, w, _ in pieces
    ]
    weight_loads = [
        load(gate_ref, w_pair.at[:, pl.ds(0, 128)]),
        load(up_ref, w_pair.at[:, pl.ds(128, 128)]),
        load(down_ref, w_down),
    ]

    barrier = pltpu.get_barrier_semaphore()
    pl.semaphore_signal(barrier, inc=1, device_id={"expert": partner}, device_id_type=MESH)

    @pl.when(not_top)
    def _():
        pl.semaphore_signal(barrier, inc=1, device_id={"expert": above}, device_id_type=MESH)

    @pl.when(not_low)
    def _():
        pl.semaphore_signal(barrier, inc=1, device_id={"expert": below}, device_id_type=MESH)

    @pl.when(to_pipe)
    def _():
        pl.semaphore_signal(barrier, inc=1, device_id={"pipe": stage - 1}, device_id_type=MESH)

    @pl.when(from_pipe)
    def _():
        pl.semaphore_signal(barrier, inc=1, device_id={"pipe": stage + 1}, device_id_type=MESH)

    def one(flag):
        return jnp.where(flag, 1, 0).astype(jnp.int32)

    pl.semaphore_wait(barrier, 1 + one(not_top) + one(not_low) + one(to_pipe) + one(from_pipe))

    sent = []

    def send(conds, src, dst, tx, rx, device):
        def make():
            return pltpu.make_async_remote_copy(
                src_ref=src(),
                dst_ref=dst(),
                send_sem=tx(),
                recv_sem=rx(),
                device_id=device,
                device_id_type=MESH,
            )

        guard(conds, lambda: make().start())
        return conds, make

    def guard(conds, run):
        if conds:
            flag = conds[0]
            for cond in conds[1:]:
                flag = flag & cond
            pl.when(flag)(run)
        else:
            run()

    def arrived(ref, tx, rx):
        pltpu.make_async_remote_copy(
            src_ref=ref,
            dst_ref=ref,
            send_sem=tx,
            recv_sem=rx,
            device_id={"expert": partner},
            device_id_type=MESH,
        ).wait_recv()

    messages = ([], [])
    number = 0
    for half in range(2):
        for array in (x_all, g_all):
            for c, w, is_wide in pieces:
                if array is g_all and c + w == width:
                    w = w + 128
                messages[half].append((half, array, c, w, is_wide, number))
                number += 1

    def gather_send(message, block, conds, tx, device):
        half, array, c, w, _, n = message
        view = lambda: array.at[rows(half, block), pl.ds(c, w)]
        sent.append(
            send(conds, view, view, lambda: tx.at[block, n], lambda: ag_rx.at[block, n], device)
        )

    def gather_wait(message, block):
        half, array, c, w, _, n = message
        view = array.at[rows(half, block), pl.ds(c, w)]
        arrived(view, ag_y.at[block, n], ag_rx.at[block, n])

    to_above = {"expert": above}
    to_below = {"expert": below}
    to_partner = {"expert": partner}
    to_prev = {"pipe": stage - 1}
    beside = z * COLS + other

    def own(half, conds, tx, device):
        for message in messages[half]:
            gather_send(message, me, conds, tx, device)

    def narrow_beside(half):
        for message in messages[half]:
            if not message[4]:
                gather_wait(message, beside)

    def pass_beside(half, conds, tx, device):
        for message in messages[half]:
            if not message[4]:
                gather_send(message, beside, conds, tx, device)

    def gather_stage(half, k):
        for message in messages[half]:
            for low in (True, False):
                at_z = z - k if low else z + k
                valid = z >= k if low else z + k <= top
                onward, tx, device = (
                    (not_top, ag_up, to_above) if low else (not_low, ag_dn, to_below)
                )
                for column in [y] if message[4] else [y, other]:
                    block = at_z * COLS + column
                    guard([valid], functools.partial(gather_wait, message, block))
                    gather_send(message, block, [valid, onward], tx, device)
                    if message[4]:
                        gather_send(message, block, [valid], ag_y, to_partner)

    def gather_end(half):
        for message in messages[half]:
            if message[4]:
                for at_z in range(top + 1):
                    gather_wait(message, at_z * COLS + other)

    picked = select_ref[...]
    for half in range(2):
        g_all[rows(half, me), pl.ds(width, 128)] = weight_ref[pl.ds(half * HALF, HALF), :]
    for first, second in zip(*messages):
        _, array, c, _, _, n = first
        at = n % count
        loads, source = (
            (layer_loads, layer_buf) if array is x_all else (upstream_loads, upstream_buf)
        )
        w = pieces[at][1]
        loads[at].wait()
        chosen = jnp.dot(
            picked, source[:, pl.ds(c, w)], preferred_element_type=jnp.float32
        ).astype(jnp.bfloat16)
        array[rows(0, me), pl.ds(c, w)] = chosen[:HALF]
        array[rows(1, me), pl.ds(c, w)] = chosen[HALF:]
        gather_send(first, me, [], ag_y, to_partner)
        gather_send(first, me, [not_top], ag_up, to_above)
        gather_send(first, me, [not_low], ag_dn, to_below)
    sent.append(
        send(
            [to_pipe],
            lambda: select_ref,
            lambda: select_out,
            lambda: pipe_tx.at[0],
            lambda: pipe_rx.at[0],
            to_prev,
        )
    )
    sent.append(
        send(
            [to_pipe],
            lambda: upstream_ref,
            lambda: behind_out,
            lambda: pipe_tx.at[1],
            lambda: pipe_rx.at[1],
            to_prev,
        )
    )

    narrow_beside(0)
    pass_beside(0, [not_top], ag_up, to_above)
    pass_beside(0, [not_low], ag_dn, to_below)
    own(1, [not_low, z == top], ag_dn, to_below)
    own(1, [not_top, z == 0], ag_up, to_above)
    for k in range(1, top + 1):
        gather_stage(0, k)
        if k < top:
            own(1, [z == top - k], ag_dn, to_below)
            own(1, [z == k], ag_up, to_above)
    own(1, [], ag_y, to_partner)
    narrow_beside(1)
    pass_beside(1, [not_top], ag_up, to_above)
    pass_beside(1, [not_low], ag_dn, to_below)

    step = width // 7

    def layer(half):
        mine = pl.ds(half * span, span)
        both[...] = jnp.zeros_like(both)
        back[...] = jnp.zeros_like(back)

        def forward(i, _):
            at = pl.ds(pl.multiple_of(i * step, 128), step)
            both[...] += jnp.dot(x_all[mine, at], w_pair[at, :], preferred_element_type=jnp.float32)
            back[...] += lax.dot_general(
                g_all[mine, at],
                w_down[:, at],
                (((1,), (1,)), ((), ())),
                preferred_element_type=jnp.float32,
            )
            return 0

        lax.fori_loop(0, 7, forward, 0)
        gate = both[:, pl.ds(0, 128)]
        up = both[:, pl.ds(128, 128)]
        raw = back[...]
        scale = g_all[mine, pl.ds(width, 128)].astype(jnp.float32)
        sigmoid = jax.nn.sigmoid(gate)
        silu = gate * sigmoid
        hidden = (silu * up).astype(jnp.bfloat16).astype(jnp.float32)
        score = jnp.sum(hidden * raw, axis=1, keepdims=True)
        part[mine, pl.ds(width, 128)] = jnp.broadcast_to(score, (span, 128)).astype(jnp.bfloat16)
        scaled = scale * raw
        pair_out[mine, pl.ds(0, 128)] = (
            scaled * up * sigmoid * (1.0 + gate * (1.0 - sigmoid))
        ).astype(jnp.bfloat16)
        pair_out[mine, pl.ds(128, 128)] = (scaled * silu).astype(jnp.bfloat16)
        hidden_out[mine, :] = (hidden * scale).astype(jnp.bfloat16)

    sum_count = max(len(p) for p in sum_pieces)

    def sum_piece(half, n):
        c, w, is_wide = sum_pieces[half][n]
        return c, w + 128 if c + w == width else w, is_wide

    def part_view(buffer, half, n, block):
        c, w, _ = sum_piece(half, n)
        return buffer.at[rows(half, block), pl.ds(c, w)]

    def part_send(half, n, block, conds, buffer, tx, rx, device):
        at = half * sum_count + n
        sent.append(
            send(
                conds,
                lambda: part_view(part, half, n, block),
                lambda: part_view(buffer, half, n, block),
                lambda: tx.at[block, at],
                lambda: rx.at[block, at],
                device,
            )
        )

    def part_wait(half, n, block, buffer, tx, rx):
        at = half * sum_count + n
        arrived(part_view(buffer, half, n, block), tx.at[block, at], rx.at[block, at])

    def back_rows(half):
        mine = pl.ds(half * span, span)
        for n, (c, w, is_wide) in enumerate(sum_pieces[half]):
            for start in range(c, c + w, 1024):
                at = pl.ds(start, min(1024, c + w - start))
                part[mine, at] = lax.dot_general(
                    pair_out[mine, :],
                    w_pair[at, :],
                    (((1,), (1,)), ((), ())),
                    preferred_element_type=jnp.float32,
                ).astype(jnp.bfloat16)
            if is_wide:
                for k in range(top, 0, -1):
                    for at_z, valid in ((z - k, z >= k), (z + k, z + k <= top)):
                        block = at_z * COLS + other
                        part_send(half, n, block, [valid], from_y, rs_y_tx, rs_y_rx, to_partner)
                part_send(half, n, beside, [], from_y, rs_y_tx, rs_y_rx, to_partner)

    def merge(half, n, block, terms):
        c, w, _ = sum_piece(half, n)
        here = (rows(half, block), pl.ds(c, w))
        temp[:, pl.ds(0, w)] = part[here].astype(jnp.float32)
        for cond, buffer, tx, rx in terms:

            def add(buffer=buffer, tx=tx, rx=rx):
                part_wait(half, n, block, buffer, tx, rx)
                temp[:, pl.ds(0, w)] += buffer[here].astype(jnp.float32)

            guard([] if cond is None else [cond], add)
        part[here] = temp[:, pl.ds(0, w)].astype(jnp.bfloat16)

    via_y = (None, from_y, rs_y_tx, rs_y_rx)
    via_above = (not_top, from_above, rs_dn_tx, rs_dn_rx)
    via_below = (not_low, from_below, rs_up_tx, rs_up_rx)

    def sum_stage(half, k):
        for n, (_, _, is_wide) in enumerate(sum_pieces[half]):
            for low in (True, False):
                at_z = z - k if low else z + k
                valid = z >= k if low else z + k <= top
                for column in [y] if is_wide else [y, other]:
                    block = at_z * COLS + column
                    via_z, edge = (via_above, not_top) if low else (via_below, not_low)
                    if is_wide:
                        guard([valid], functools.partial(merge, half, n, block, [via_y, via_z]))
                    else:
                        only = [(None,) + via_z[1:]]
                        guard([valid, edge], functools.partial(merge, half, n, block, only))
                    if low:
                        out = (from_above, rs_dn_tx, rs_dn_rx, to_below)
                    else:
                        out = (from_below, rs_up_tx, rs_up_rx, to_above)
                    part_send(half, n, block, [valid], *out)

    def sum_end(half):
        for n, (_, _, is_wide) in enumerate(sum_pieces[half]):
            if not is_wide:
                merge(half, n, beside, [via_above, via_below])
                part_send(half, n, beside, [], from_y, rs_y_tx, rs_y_rx, to_partner)
        for n, (c, w, is_wide) in enumerate(sum_pieces[half]):
            merge(half, n, me, [via_above, via_below, via_y])
            at = 2 + half * sum_count + n
            sent.append(
                send(
                    [to_pipe],
                    lambda c=c, w=w: part.at[rows(half, me), pl.ds(c, w)],
                    lambda c=c, w=w: sums_out.at[pl.ds(half * HALF, HALF), pl.ds(c, w)],
                    lambda at=at: pipe_tx.at[at],
                    lambda at=at: pipe_rx.at[at],
                    to_prev,
                )
            )
        score_out[pl.ds(half * HALF, HALF), :] = part[rows(half, me), pl.ds(width, 128)].astype(
            jnp.float32
        )

    gather_stage(1, 1)
    gather_end(0)
    for copy in weight_loads:
        copy.wait()
    layer(0)
    back_rows(0)
    sum_stage(0, top)
    gather_stage(1, 2)
    sum_stage(0, 2)
    gather_stage(1, 3)
    sum_stage(0, 1)
    gather_end(1)
    rows_copy = load(x_all, rows_out)
    grads_copy = load(g_all.at[:, pl.ds(0, width)], grads_out)
    layer(1)
    back_rows(1)
    sum_stage(1, top)
    sum_end(0)
    sum_stage(1, 2)
    sum_stage(1, 1)
    sum_end(1)

    @pl.when(from_pipe)
    def _():
        arrived(select_out, pipe_tx.at[0], pipe_rx.at[0])
        arrived(behind_out, pipe_tx.at[1], pipe_rx.at[1])
        for half in range(2):
            for n, (c, w, _) in enumerate(sum_pieces[half]):
                at = 2 + half * sum_count + n
                view = sums_out.at[pl.ds(half * HALF, HALF), pl.ds(c, w)]
                arrived(view, pipe_tx.at[at], pipe_rx.at[at])

    for conds, make in sent:
        guard(conds, lambda make=make: make().wait_send())
    rows_copy.wait()
    grads_copy.wait()


def finish(
    keep, x, g, pair, hidden, behind, select, sums, prev_out, gate_out, up_out, down_out
):
    first = (((0,), (0,)), ((), ()))
    grads = lax.dot_general(x[...], pair[...], first, preferred_element_type=jnp.float32)
    gate_out[...] = grads[:, :128].astype(jnp.bfloat16)
    up_out[...] = grads[:, 128:].astype(jnp.bfloat16)
    down_out[...] = lax.dot_general(
        hidden[...], g[...], first, preferred_element_type=jnp.float32
    ).astype(jnp.bfloat16)
    moved = lax.dot_general(select[...], sums[...], first, preferred_element_type=jnp.float32)
    prev = behind[...].astype(jnp.float32) + moved
    prev_out[...] = jnp.where(keep[0] > 0, prev, 0.0).astype(jnp.bfloat16)


def fused(
    pipes,
    layer_input,
    output_grad,
    gate_weight,
    up_weight,
    down_weight,
    expert_ids,
    slots,
    combine_weights,
):
    _, tokens, width = layer_input.shape
    half = jnp.bfloat16
    units = gate_weight.shape[2]
    total = GROUP * CAP
    routes, places = expert_ids[0], slots[0]
    usable = (routes < 1) & (places < CAP)
    positions = jnp.where(usable, routes * CAP + places, CAP)
    hits = positions.T[:, None, :] == lax.broadcasted_iota(jnp.int32, (1, CAP, 1), 1)
    select = jnp.sum(hits.astype(jnp.float32), axis=0).astype(half)
    weight = jnp.sum(
        jnp.where(hits, combine_weights[0].astype(jnp.float32).T[:, None, :], 0.0), axis=(0, 2)
    )
    weight = jnp.broadcast_to(weight.astype(half)[:, None], (CAP, 128))
    pieces, sum_pieces = plan(width)
    count = len(pieces)
    sum_count = max(len(p) for p in sum_pieces)
    widest = max(w for p in sum_pieces for _, w, _ in p) + 128
    dma = pltpu.SemaphoreType.DMA
    vmem = pl.BlockSpec(memory_space=pltpu.VMEM)
    hbm = pl.BlockSpec(memory_space=pl.ANY)
    shape = jax.ShapeDtypeStruct
    x_all, g_all, pair, hidden, behind, select_next, sums, score = pl.pallas_call(
        functools.partial(exchange, pipes),
        out_shape=(
            shape((total, width), half),
            shape((total, width), half),
            shape((total, 2 * units), half),
            shape((total, units), half),
            shape((tokens, width), half),
            shape((CAP, tokens), half),
            shape((CAP, width), half),
            shape((CAP, 128), jnp.float32),
        ),
        in_specs=[hbm, hbm, hbm, hbm, hbm, vmem, vmem],
        out_specs=(hbm, hbm, vmem, vmem, hbm, hbm, hbm, vmem),
        scratch_shapes=[
            pltpu.VMEM((tokens, width), half),
            pltpu.VMEM((tokens, width), half),
            pltpu.VMEM((total, width), half),
            pltpu.VMEM((total, width + 128), half),
            pltpu.VMEM((width, 2 * units), half),
            pltpu.VMEM((units, width), half),
            pltpu.VMEM((total, width + 128), half),
            pltpu.VMEM((total, width + 128), half),
            pltpu.VMEM((total, width + 128), half),
            pltpu.VMEM((total, width + 128), half),
            pltpu.VMEM((total // 2, 2 * units), jnp.float32),
            pltpu.VMEM((total // 2, units), jnp.float32),
            pltpu.VMEM((HALF, widest), jnp.float32),
            dma((2 * count + 5,)),
            *[dma((GROUP, 4 * count)) for _ in range(4)],
            *[dma((GROUP, 2 * sum_count)) for _ in range(6)],
            dma((2 + 2 * sum_count,)),
            dma((2 + 2 * sum_count,)),
        ],
        compiler_params=pltpu.CompilerParams(
            collective_id=0, has_side_effects=True, vmem_limit_bytes=60 * 1024 * 1024
        ),
        name="exchange",
    )(
        layer_input[0],
        output_grad[0],
        gate_weight[0],
        up_weight[0],
        down_weight[0],
        select,
        weight,
    )
    keep = jnp.where(lax.axis_index("pipe") < pipes - 1, 1, 0).astype(jnp.int32).reshape(1)
    tile = width // 7
    across = lambda height: pl.BlockSpec((height, tile), lambda i: (0, i))
    along = pl.BlockSpec((tile, units), lambda i: (i, 0))
    whole = lambda *dims: pl.BlockSpec(dims, lambda i: (0, 0))
    prev, gate_grad, up_grad, down_grad = pl.pallas_call(
        finish,
        grid=(7,),
        out_shape=(
            shape((tokens, width), half),
            shape((width, units), half),
            shape((width, units), half),
            shape((units, width), half),
        ),
        in_specs=[
            pl.BlockSpec(memory_space=pltpu.SMEM),
            across(total),
            across(total),
            whole(total, 2 * units),
            whole(total, units),
            across(tokens),
            whole(CAP, tokens),
            across(CAP),
        ],
        out_specs=(across(tokens), along, along, across(units)),
        compiler_params=pltpu.CompilerParams(vmem_limit_bytes=60 * 1024 * 1024),
        name="finish",
    )(keep, x_all, g_all, pair, hidden, behind, select_next, sums)
    router_grad = jnp.sum(jnp.where(hits, score[:, 0][None, :, None], 0.0), axis=1).T
    return (prev[None], gate_grad[None], up_grad[None], down_grad[None], router_grad[None])


def solution(mesh):
    body = shards
    if mesh.shape["expert"] == GROUP:
        body = functools.partial(fused, mesh.shape["pipe"])
    return jax.shard_map(
        body,
        mesh=mesh,
        in_specs=(
            P("pipe", "expert", None),
            P("pipe", "expert", None),
            P("pipe", None, "expert"),
            P("pipe", None, "expert"),
            P("pipe", "expert", None),
            P("pipe", "expert", None),
            P("pipe", "expert", None),
            P("pipe", "expert", None),
        ),
        out_specs=(
            P("pipe", "expert", None),
            P("pipe", None, "expert"),
            P("pipe", None, "expert"),
            P("pipe", "expert", None),
            P("pipe", "expert", None),
        ),
        check_vma=False,
    )
```

```python
import functools

import jax
import jax.numpy as jnp
from jax import lax
from jax.experimental import pallas as pl
from jax.experimental.pallas import tpu as pltpu
from jax.sharding import PartitionSpec as P

GROUP = 8
CAP = 32
COLS = 2
HALF = CAP // 2
MESH = pl.DeviceIdType.MESH


def from_behind(x, axis, by):
    size = lax.axis_size(axis)
    pairs = [(i, i + by) for i in range(size) if 0 <= i + by < size]
    return lax.ppermute(x, axis, pairs)


def shards(
    layer_input,
    output_grad,
    gate_weight,
    up_weight,
    down_weight,
    expert_ids,
    slots,
    combine_weights,
):
    devices = lax.axis_size("expert")
    window = devices // GROUP
    width = layer_input.shape[2]
    inputs = layer_input[0]
    upstream_grad = output_grad[0]
    w_gate = gate_weight[0]
    w_up = up_weight[0]
    w_down = down_weight[0]
    routes = expert_ids[0]
    places = slots[0]
    positions = routes * CAP + places
    usable = (routes < window) & (places < CAP)
    columns = lax.broadcasted_iota(jnp.int32, (1, 1, window * CAP), 2)
    picker = ((positions[:, :, None] == columns) & usable[:, :, None]).astype(jnp.float32)
    selection = jnp.sum(picker, axis=1)
    select_half = selection.astype(jnp.bfloat16)
    contract_first = (((0,), (0,)), ((), ()))
    contract_last = (((1,), (1,)), ((), ()))
    token_buffer = lax.dot_general(
        select_half, inputs, contract_first, preferred_element_type=jnp.float32
    ).astype(jnp.bfloat16)
    grad_buffer = lax.dot_general(
        select_half, upstream_grad, contract_first, preferred_element_type=jnp.float32
    ).astype(jnp.bfloat16)
    weight_buffer = jnp.einsum("tkp,tk->p", picker, combine_weights[0].astype(jnp.float32)).astype(
        jnp.bfloat16
    )
    token_blocks = token_buffer.reshape(window, CAP, width)
    grad_blocks = grad_buffer.reshape(window, CAP, width)
    weight_blocks = weight_buffer.reshape(window, CAP)
    collected = (
        lax.all_gather(token_blocks, "expert", axis=0, tiled=True),
        lax.all_gather(grad_blocks, "expert", axis=0, tiled=True),
        lax.all_gather(weight_blocks, "expert", axis=0, tiled=True),
    )
    owner = lax.axis_index("expert") // GROUP
    expert_rows = lax.dynamic_index_in_dim(
        collected[0].reshape(devices, window, CAP, width), owner, 1, False
    )
    expert_grads = lax.dynamic_index_in_dim(
        collected[1].reshape(devices, window, CAP, width), owner, 1, False
    )
    expert_weights = lax.dynamic_index_in_dim(
        collected[2].reshape(devices, window, CAP), owner, 1, False
    )
    flat_rows = expert_rows.reshape(devices * CAP, width)
    flat_grads = expert_grads.reshape(devices * CAP, width)
    flat_weights = expert_weights.reshape(devices * CAP, 1)
    gate_pre = jnp.dot(flat_rows, w_gate, preferred_element_type=jnp.float32)
    up_pre = jnp.dot(flat_rows, w_up, preferred_element_type=jnp.float32)
    sigmoid_gate = jax.nn.sigmoid(gate_pre)
    silu_gate = gate_pre * sigmoid_gate
    hidden = (silu_gate * up_pre).astype(jnp.bfloat16)
    scaled = (flat_weights.astype(jnp.float32) * flat_grads.astype(jnp.float32)).astype(
        jnp.bfloat16
    )
    partial_out = jnp.dot(hidden, w_down, preferred_element_type=jnp.float32)
    score_part = jnp.sum(partial_out * flat_grads.astype(jnp.float32), axis=1)
    back_hidden = lax.dot_general(scaled, w_down, contract_last, preferred_element_type=jnp.float32)
    dgate = (back_hidden * up_pre * sigmoid_gate * (1.0 + gate_pre * (1.0 - sigmoid_gate))).astype(
        jnp.bfloat16
    )
    dup = (back_hidden * silu_gate).astype(jnp.bfloat16)
    down_grad = lax.dot_general(
        hidden, scaled, contract_first, preferred_element_type=jnp.float32
    ).astype(jnp.bfloat16)
    gate_grad = lax.dot_general(
        flat_rows, dgate, contract_first, preferred_element_type=jnp.float32
    ).astype(jnp.bfloat16)
    up_grad = lax.dot_general(
        flat_rows, dup, contract_first, preferred_element_type=jnp.float32
    ).astype(jnp.bfloat16)
    back_input = lax.dot_general(dgate, w_gate, contract_last, preferred_element_type=jnp.float32)
    back_input = back_input + lax.dot_general(
        dup, w_up, contract_last, preferred_element_type=jnp.float32
    )
    back_half = back_input.astype(jnp.bfloat16)
    owner = lax.axis_index("expert") // GROUP
    placing = (lax.broadcasted_iota(jnp.int32, (1, window, 1), 1) == owner).astype(jnp.float32)
    back_terms = (
        back_half.reshape(devices, 1, CAP, width) * placing.astype(jnp.bfloat16)[:, :, :, None]
    )
    score_terms = score_part.reshape(devices, 1, CAP) * placing
    summed, score_summed = (
        lax.psum_scatter(back_terms, "expert", scatter_dimension=0, tiled=True).astype(jnp.float32),
        lax.psum_scatter(
            score_terms.astype(jnp.bfloat16), "expert", scatter_dimension=0, tiled=True
        ).astype(jnp.float32),
    )
    grouped = summed.reshape(window * CAP, width)
    score_sum = score_summed.reshape(window * CAP)
    contribution = jnp.dot(selection, grouped, precision=lax.Precision.HIGHEST)
    input_grad = (upstream_grad.astype(jnp.float32) + contribution).astype(jnp.bfloat16)
    router_grad = jnp.einsum("tkp,p->tk", picker, score_sum, precision=lax.Precision.HIGHEST)
    previous = from_behind(input_grad[None], "pipe", -1)
    return (previous, gate_grad[None], up_grad[None], down_grad[None], router_grad[None])


def cuts(width, shares, narrow_count):
    unit = width // 7 // 128 * 128
    pieces, at = [], 0
    for share in shares:
        pieces.append((at, share * unit, True))
        at += share * unit
    step = (width - at) // narrow_count // 128 * 128
    narrow = []
    for i in range(narrow_count):
        w = step if i < narrow_count - 1 else width - at
        narrow.append((at, w, False))
        at += w
    return narrow + pieces


def plan(width):
    gather = cuts(width, (3, 3), 1)
    return gather, (cuts(width, (2,), 2), cuts(width, (2, 2, 2), 1))


def hits_of(routes, places, k):
    route, place = routes[pl.ds(k, 1), :], places[pl.ds(k, 1), :]
    position = jnp.where((route < 1) & (place < CAP), route * CAP + place, CAP)
    return position == lax.broadcasted_iota(jnp.int32, (CAP, routes.shape[1]), 0)


def exchange(
    pipes,
    layer_ref,
    upstream_ref,
    gate_ref,
    up_ref,
    down_ref,
    routes_ref,
    places_ref,
    combine_ref,
    rows_out,
    grads_out,
    pair_out,
    hidden_out,
    behind_out,
    select_out,
    sums_out,
    score_out,
    select_ref,
    layer_buf,
    upstream_buf,
    x_all,
    g_all,
    w_pair,
    w_down,
    part,
    from_y,
    from_above,
    from_below,
    both,
    back,
    temp,
    local_sem,
    ag_rx,
    ag_up,
    ag_dn,
    ag_y,
    rs_y_tx,
    rs_y_rx,
    rs_up_tx,
    rs_up_rx,
    rs_dn_tx,
    rs_dn_rx,
    pipe_tx,
    pipe_rx,
):
    me = lax.axis_index("expert")
    stage = lax.axis_index("pipe")
    y = lax.rem(me, COLS)
    z = lax.div(me, COLS)
    top = GROUP // COLS - 1
    other = 1 - y
    partner = me + 1 - 2 * y
    above, below = me + COLS, me - COLS
    width = layer_ref.shape[1]
    total = x_all.shape[0]
    pieces, sum_pieces = plan(width)
    count = len(pieces)
    span = total // 2
    not_top, not_low = z < top, z > 0
    to_pipe, from_pipe = stage > 0, stage < pipes - 1

    def rows(half, block):
        return pl.ds(pl.multiple_of(half * span + block * HALF, HALF), HALF)

    local = []

    def load(src, dst):
        copy = pltpu.make_async_copy(src, dst, local_sem.at[len(local)])
        local.append(copy)
        copy.start()
        return copy

    layer_loads = [
        load(layer_ref.at[:, pl.ds(c, w)], layer_buf.at[:, pl.ds(c, w)]) for c, w, _ in pieces
    ]
    upstream_loads = [
        load(upstream_ref.at[:, pl.ds(c, w)], upstream_buf.at[:, pl.ds(c, w)]) for c, w, _ in pieces
    ]
    weight_loads = [
        load(gate_ref, w_pair.at[:, pl.ds(0, 128)]),
        load(up_ref, w_pair.at[:, pl.ds(128, 128)]),
        load(down_ref, w_down),
    ]

    picked = jnp.zeros(select_ref.shape, jnp.float32)
    weight = jnp.zeros(select_ref.shape, jnp.float32)
    for k in range(routes_ref.shape[0]):
        hit = hits_of(routes_ref, places_ref, k)
        picked = picked + jnp.where(hit, 1.0, 0.0)
        combine = combine_ref[pl.ds(k, 1), :].astype(jnp.float32)
        weight = weight + jnp.where(hit, combine, 0.0)
    select_ref[...] = picked.astype(jnp.bfloat16)
    weight = jnp.broadcast_to(jnp.sum(weight, axis=1, keepdims=True), (CAP, 128))
    weight = weight.astype(jnp.bfloat16)

    barrier = pltpu.get_barrier_semaphore()
    pl.semaphore_signal(barrier, inc=1, device_id={"expert": partner}, device_id_type=MESH)

    @pl.when(not_top)
    def _():
        pl.semaphore_signal(barrier, inc=1, device_id={"expert": above}, device_id_type=MESH)

    @pl.when(not_low)
    def _():
        pl.semaphore_signal(barrier, inc=1, device_id={"expert": below}, device_id_type=MESH)

    @pl.when(to_pipe)
    def _():
        pl.semaphore_signal(barrier, inc=1, device_id={"pipe": stage - 1}, device_id_type=MESH)

    @pl.when(from_pipe)
    def _():
        pl.semaphore_signal(barrier, inc=1, device_id={"pipe": stage + 1}, device_id_type=MESH)

    def one(flag):
        return jnp.where(flag, 1, 0).astype(jnp.int32)

    pl.semaphore_wait(barrier, 1 + one(not_top) + one(not_low) + one(to_pipe) + one(from_pipe))

    sent = []

    def send(conds, src, dst, tx, rx, device):
        def make():
            return pltpu.make_async_remote_copy(
                src_ref=src(),
                dst_ref=dst(),
                send_sem=tx(),
                recv_sem=rx(),
                device_id=device,
                device_id_type=MESH,
            )

        guard(conds, lambda: make().start())
        return conds, make

    def guard(conds, run):
        if conds:
            flag = conds[0]
            for cond in conds[1:]:
                flag = flag & cond
            pl.when(flag)(run)
        else:
            run()

    def arrived(ref, tx, rx):
        pltpu.make_async_remote_copy(
            src_ref=ref,
            dst_ref=ref,
            send_sem=tx,
            recv_sem=rx,
            device_id={"expert": partner},
            device_id_type=MESH,
        ).wait_recv()

    messages = ([], [])
    number = 0
    for half in range(2):
        for array in (x_all, g_all):
            for c, w, is_wide in pieces:
                if array is g_all and c + w == width:
                    w = w + 128
                messages[half].append((half, array, c, w, is_wide, number))
                number += 1

    def gather_send(message, block, conds, tx, device):
        half, array, c, w, _, n = message
        view = lambda: array.at[rows(half, block), pl.ds(c, w)]
        sent.append(
            send(conds, view, view, lambda: tx.at[block, n], lambda: ag_rx.at[block, n], device)
        )

    def gather_wait(message, block):
        half, array, c, w, _, n = message
        view = array.at[rows(half, block), pl.ds(c, w)]
        arrived(view, ag_y.at[block, n], ag_rx.at[block, n])

    to_above = {"expert": above}
    to_below = {"expert": below}
    to_partner = {"expert": partner}
    to_prev = {"pipe": stage - 1}
    beside = z * COLS + other

    def own(half, conds, tx, device):
        for message in messages[half]:
            gather_send(message, me, conds, tx, device)

    def narrow_beside(half):
        for message in messages[half]:
            if not message[4]:
                gather_wait(message, beside)

    def pass_beside(half, conds, tx, device):
        for message in messages[half]:
            if not message[4]:
                gather_send(message, beside, conds, tx, device)

    def gather_stage(half, k):
        for message in messages[half]:
            for low in (True, False):
                at_z = z - k if low else z + k
                valid = z >= k if low else z + k <= top
                onward, tx, device = (
                    (not_top, ag_up, to_above) if low else (not_low, ag_dn, to_below)
                )
                for column in [y] if message[4] else [y, other]:
                    block = at_z * COLS + column
                    guard([valid], functools.partial(gather_wait, message, block))
                    gather_send(message, block, [valid, onward], tx, device)
                    if message[4]:
                        gather_send(message, block, [valid], ag_y, to_partner)

    def gather_end(half):
        for message in messages[half]:
            if message[4]:
                for at_z in range(top + 1):
                    gather_wait(message, at_z * COLS + other)

    picked = select_ref[...]
    for half in range(2):
        g_all[rows(half, me), pl.ds(width, 128)] = weight[half * HALF : (half + 1) * HALF]
    for first, second in zip(*messages):
        _, array, c, _, _, n = first
        at = n % count
        loads, source = (
            (layer_loads, layer_buf) if array is x_all else (upstream_loads, upstream_buf)
        )
        w = pieces[at][1]
        loads[at].wait()
        chosen = jnp.dot(
            picked, source[:, pl.ds(c, w)], preferred_element_type=jnp.float32
        ).astype(jnp.bfloat16)
        array[rows(0, me), pl.ds(c, w)] = chosen[:HALF]
        array[rows(1, me), pl.ds(c, w)] = chosen[HALF:]
        gather_send(first, me, [], ag_y, to_partner)
        gather_send(first, me, [not_top], ag_up, to_above)
        gather_send(first, me, [not_low], ag_dn, to_below)
    sent.append(
        send(
            [to_pipe],
            lambda: select_ref,
            lambda: select_out,
            lambda: pipe_tx.at[0],
            lambda: pipe_rx.at[0],
            to_prev,
        )
    )
    sent.append(
        send(
            [to_pipe],
            lambda: upstream_ref,
            lambda: behind_out,
            lambda: pipe_tx.at[1],
            lambda: pipe_rx.at[1],
            to_prev,
        )
    )

    narrow_beside(0)
    pass_beside(0, [not_top], ag_up, to_above)
    pass_beside(0, [not_low], ag_dn, to_below)
    own(1, [not_low, z == top], ag_dn, to_below)
    own(1, [not_top, z == 0], ag_up, to_above)
    for k in range(1, top + 1):
        gather_stage(0, k)
        if k < top:
            own(1, [z == top - k], ag_dn, to_below)
            own(1, [z == k], ag_up, to_above)
    own(1, [], ag_y, to_partner)
    narrow_beside(1)
    pass_beside(1, [not_top], ag_up, to_above)
    pass_beside(1, [not_low], ag_dn, to_below)

    step = width // 7

    def layer(half):
        mine = pl.ds(half * span, span)
        both[...] = jnp.zeros_like(both)
        back[...] = jnp.zeros_like(back)

        def forward(i, _):
            at = pl.ds(pl.multiple_of(i * step, 128), step)
            both[...] += jnp.dot(x_all[mine, at], w_pair[at, :], preferred_element_type=jnp.float32)
            back[...] += lax.dot_general(
                g_all[mine, at],
                w_down[:, at],
                (((1,), (1,)), ((), ())),
                preferred_element_type=jnp.float32,
            )
            return 0

        lax.fori_loop(0, 7, forward, 0)
        gate = both[:, pl.ds(0, 128)]
        up = both[:, pl.ds(128, 128)]
        raw = back[...]
        scale = g_all[mine, pl.ds(width, 128)].astype(jnp.float32)
        sigmoid = jax.nn.sigmoid(gate)
        silu = gate * sigmoid
        hidden = (silu * up).astype(jnp.bfloat16).astype(jnp.float32)
        score = jnp.sum(hidden * raw, axis=1, keepdims=True)
        part[mine, pl.ds(width, 128)] = jnp.broadcast_to(score, (span, 128)).astype(jnp.bfloat16)
        scaled = scale * raw
        pair_out[mine, pl.ds(0, 128)] = (
            scaled * up * sigmoid * (1.0 + gate * (1.0 - sigmoid))
        ).astype(jnp.bfloat16)
        pair_out[mine, pl.ds(128, 128)] = (scaled * silu).astype(jnp.bfloat16)
        hidden_out[mine, :] = (hidden * scale).astype(jnp.bfloat16)

    sum_count = max(len(p) for p in sum_pieces)

    def sum_piece(half, n):
        c, w, is_wide = sum_pieces[half][n]
        return c, w + 128 if c + w == width else w, is_wide

    def part_view(buffer, half, n, block):
        c, w, _ = sum_piece(half, n)
        return buffer.at[rows(half, block), pl.ds(c, w)]

    def part_send(half, n, block, conds, buffer, tx, rx, device):
        at = half * sum_count + n
        sent.append(
            send(
                conds,
                lambda: part_view(part, half, n, block),
                lambda: part_view(buffer, half, n, block),
                lambda: tx.at[block, at],
                lambda: rx.at[block, at],
                device,
            )
        )

    def part_wait(half, n, block, buffer, tx, rx):
        at = half * sum_count + n
        arrived(part_view(buffer, half, n, block), tx.at[block, at], rx.at[block, at])

    def back_piece(half, n):
        mine = pl.ds(half * span, span)
        c, w, _ = sum_pieces[half][n]
        for start in range(c, c + w, 1024):
            at = pl.ds(start, min(1024, c + w - start))
            part[mine, at] = lax.dot_general(
                pair_out[mine, :],
                w_pair[at, :],
                (((1,), (1,)), ((), ())),
                preferred_element_type=jnp.float32,
            ).astype(jnp.bfloat16)

    def over_y(half, n, k):
        if k == 0:
            part_send(half, n, beside, [], from_y, rs_y_tx, rs_y_rx, to_partner)
        else:
            for at_z, valid in ((z - k, z >= k), (z + k, z + k <= top)):
                block = at_z * COLS + other
                part_send(half, n, block, [valid], from_y, rs_y_tx, rs_y_rx, to_partner)

    def back_narrow(half):
        for n, (_, _, is_wide) in enumerate(sum_pieces[half]):
            if not is_wide:
                back_piece(half, n)

    def back_wide(half):
        wide = [n for n, p in enumerate(sum_pieces[half]) if p[2]]
        for n in wide:
            back_piece(half, n)
            over_y(half, n, top)
        for k in range(top - 1, -1, -1):
            for n in wide:
                over_y(half, n, k)

    def merge(half, n, block, terms):
        c, w, _ = sum_piece(half, n)
        here = (rows(half, block), pl.ds(c, w))
        temp[:, pl.ds(0, w)] = part[here].astype(jnp.float32)
        for cond, buffer, tx, rx in terms:

            def add(buffer=buffer, tx=tx, rx=rx):
                part_wait(half, n, block, buffer, tx, rx)
                temp[:, pl.ds(0, w)] += buffer[here].astype(jnp.float32)

            guard([] if cond is None else [cond], add)
        part[here] = temp[:, pl.ds(0, w)].astype(jnp.bfloat16)

    via_y = (None, from_y, rs_y_tx, rs_y_rx)
    via_above = (not_top, from_above, rs_dn_tx, rs_dn_rx)
    via_below = (not_low, from_below, rs_up_tx, rs_up_rx)

    def sum_stage(half, k, kind):
        for n, (_, _, is_wide) in enumerate(sum_pieces[half]):
            if is_wide != kind:
                continue
            for low in (True, False):
                at_z = z - k if low else z + k
                valid = z >= k if low else z + k <= top
                for column in [y] if is_wide else [y, other]:
                    block = at_z * COLS + column
                    via_z, edge = (via_above, not_top) if low else (via_below, not_low)
                    if is_wide:
                        guard([valid], functools.partial(merge, half, n, block, [via_y, via_z]))
                    else:
                        only = [(None,) + via_z[1:]]
                        guard([valid, edge], functools.partial(merge, half, n, block, only))
                    if low:
                        out = (from_above, rs_dn_tx, rs_dn_rx, to_below)
                    else:
                        out = (from_below, rs_up_tx, rs_up_rx, to_above)
                    part_send(half, n, block, [valid], *out)

    def sum_beside(half):
        for n, (_, _, is_wide) in enumerate(sum_pieces[half]):
            if not is_wide:
                merge(half, n, beside, [via_above, via_below])
                part_send(half, n, beside, [], from_y, rs_y_tx, rs_y_rx, to_partner)

    def sum_end(half):
        for n, (c, w, is_wide) in enumerate(sum_pieces[half]):
            merge(half, n, me, [via_above, via_below, via_y])
            at = 2 + half * sum_count + n
            sent.append(
                send(
                    [to_pipe],
                    lambda c=c, w=w: part.at[rows(half, me), pl.ds(c, w)],
                    lambda c=c, w=w: sums_out.at[pl.ds(half * HALF, HALF), pl.ds(c, w)],
                    lambda at=at: pipe_tx.at[at],
                    lambda at=at: pipe_rx.at[at],
                    to_prev,
                )
            )
        score_out[pl.ds(half * HALF, HALF), :] = part[rows(half, me), pl.ds(width, 128)].astype(
            jnp.float32
        )

    narrow_kind, wide_kind = False, True
    gather_stage(1, 1)
    gather_end(0)
    for copy in weight_loads:
        copy.wait()
    layer(0)
    back_narrow(0)
    sum_stage(0, top, narrow_kind)
    back_wide(0)
    gather_stage(1, 2)
    sum_stage(0, 2, narrow_kind)
    sum_stage(0, top, wide_kind)
    sum_stage(0, 1, narrow_kind)
    gather_stage(1, top)
    sum_stage(0, 2, wide_kind)
    sum_stage(0, 1, wide_kind)
    gather_end(1)
    rows_copy = load(x_all, rows_out)
    grads_copy = load(g_all.at[:, pl.ds(0, width)], grads_out)
    sum_beside(0)
    layer(1)
    back_narrow(1)
    sum_stage(1, top, narrow_kind)
    back_wide(1)
    sum_stage(1, 2, narrow_kind)
    sum_stage(1, top, wide_kind)
    sum_stage(1, 1, narrow_kind)
    sum_stage(1, 2, wide_kind)
    sum_beside(1)
    sum_stage(1, 1, wide_kind)
    sum_end(0)
    sum_end(1)

    @pl.when(from_pipe)
    def _():
        arrived(select_out, pipe_tx.at[0], pipe_rx.at[0])
        arrived(behind_out, pipe_tx.at[1], pipe_rx.at[1])
        for half in range(2):
            for n, (c, w, _) in enumerate(sum_pieces[half]):
                at = 2 + half * sum_count + n
                view = sums_out.at[pl.ds(half * HALF, HALF), pl.ds(c, w)]
                arrived(view, pipe_tx.at[at], pipe_rx.at[at])

    for conds, make in sent:
        guard(conds, lambda make=make: make().wait_send())
    rows_copy.wait()
    grads_copy.wait()


def finish(
    keep,
    routes,
    places,
    score,
    x,
    g,
    pair,
    hidden,
    behind,
    select,
    sums,
    prev_out,
    gate_out,
    up_out,
    down_out,
    router_out,
):
    @pl.when(pl.program_id(0) == 0)
    def _():
        for k in range(routes.shape[0]):
            named = jnp.where(hits_of(routes, places, k), score[:, :1], 0.0)
            router_out[pl.ds(k, 1), :] = jnp.sum(named, axis=0, keepdims=True)

    first = (((0,), (0,)), ((), ()))
    grads = lax.dot_general(x[...], pair[...], first, preferred_element_type=jnp.float32)
    gate_out[...] = grads[:, :128].astype(jnp.bfloat16)
    up_out[...] = grads[:, 128:].astype(jnp.bfloat16)
    down_out[...] = lax.dot_general(
        hidden[...], g[...], first, preferred_element_type=jnp.float32
    ).astype(jnp.bfloat16)
    moved = lax.dot_general(select[...], sums[...], first, preferred_element_type=jnp.float32)
    prev = behind[...].astype(jnp.float32) + moved
    prev_out[...] = jnp.where(keep[0] > 0, prev, 0.0).astype(jnp.bfloat16)


def fused(
    pipes,
    layer_input,
    output_grad,
    gate_weight,
    up_weight,
    down_weight,
    expert_ids,
    slots,
    combine_weights,
):
    _, tokens, width = layer_input.shape
    half = jnp.bfloat16
    units = gate_weight.shape[2]
    total = GROUP * CAP
    routes, places, combine = expert_ids[0].T, slots[0].T, combine_weights[0].T
    pieces, sum_pieces = plan(width)
    count = len(pieces)
    sum_count = max(len(p) for p in sum_pieces)
    widest = max(w for p in sum_pieces for _, w, _ in p) + 128
    dma = pltpu.SemaphoreType.DMA
    vmem = pl.BlockSpec(memory_space=pltpu.VMEM)
    hbm = pl.BlockSpec(memory_space=pl.ANY)
    shape = jax.ShapeDtypeStruct
    x_all, g_all, pair, hidden, behind, select_next, sums, score = pl.pallas_call(
        functools.partial(exchange, pipes),
        out_shape=(
            shape((total, width), half),
            shape((total, width), half),
            shape((total, 2 * units), half),
            shape((total, units), half),
            shape((tokens, width), half),
            shape((CAP, tokens), half),
            shape((CAP, width), half),
            shape((CAP, 128), jnp.float32),
        ),
        in_specs=[hbm, hbm, hbm, hbm, hbm, vmem, vmem, vmem],
        out_specs=(hbm, hbm, vmem, vmem, hbm, hbm, hbm, vmem),
        scratch_shapes=[
            pltpu.VMEM((CAP, tokens), half),
            pltpu.VMEM((tokens, width), half),
            pltpu.VMEM((tokens, width), half),
            pltpu.VMEM((total, width), half),
            pltpu.VMEM((total, width + 128), half),
            pltpu.VMEM((width, 2 * units), half),
            pltpu.VMEM((units, width), half),
            pltpu.VMEM((total, width + 128), half),
            pltpu.VMEM((total, width + 128), half),
            pltpu.VMEM((total, width + 128), half),
            pltpu.VMEM((total, width + 128), half),
            pltpu.VMEM((total // 2, 2 * units), jnp.float32),
            pltpu.VMEM((total // 2, units), jnp.float32),
            pltpu.VMEM((HALF, widest), jnp.float32),
            dma((2 * count + 5,)),
            *[dma((GROUP, 4 * count)) for _ in range(4)],
            *[dma((GROUP, 2 * sum_count)) for _ in range(6)],
            dma((2 + 2 * sum_count,)),
            dma((2 + 2 * sum_count,)),
        ],
        compiler_params=pltpu.CompilerParams(
            collective_id=0, has_side_effects=True, vmem_limit_bytes=60 * 1024 * 1024
        ),
        name="exchange",
    )(
        layer_input[0],
        output_grad[0],
        gate_weight[0],
        up_weight[0],
        down_weight[0],
        routes,
        places,
        combine,
    )
    keep = jnp.where(lax.axis_index("pipe") < pipes - 1, 1, 0).astype(jnp.int32).reshape(1)
    steps = 14
    tile = width // steps
    across = lambda height: pl.BlockSpec((height, tile), lambda i: (0, i))
    along = pl.BlockSpec((tile, units), lambda i: (i, 0))
    whole = lambda *dims: pl.BlockSpec(dims, lambda i: (0, 0))
    prev, gate_grad, up_grad, down_grad, router = pl.pallas_call(
        finish,
        grid=(steps,),
        out_shape=(
            shape((tokens, width), half),
            shape((width, units), half),
            shape((width, units), half),
            shape((units, width), half),
            shape(routes.shape, jnp.float32),
        ),
        in_specs=[
            pl.BlockSpec(memory_space=pltpu.SMEM),
            whole(*routes.shape),
            whole(*routes.shape),
            whole(CAP, 128),
            across(total),
            across(total),
            whole(total, 2 * units),
            whole(total, units),
            across(tokens),
            whole(CAP, tokens),
            across(CAP),
        ],
        out_specs=(across(tokens), along, along, across(units), whole(*routes.shape)),
        compiler_params=pltpu.CompilerParams(vmem_limit_bytes=60 * 1024 * 1024),
        name="finish",
    )(keep, routes, places, score, x_all, g_all, pair, hidden, behind, select_next, sums)
    return (prev[None], gate_grad[None], up_grad[None], down_grad[None], router.T[None])


def solution(mesh):
    body = shards
    if mesh.shape["expert"] == GROUP:
        body = functools.partial(fused, mesh.shape["pipe"])
    return jax.shard_map(
        body,
        mesh=mesh,
        in_specs=(
            P("pipe", "expert", None),
            P("pipe", "expert", None),
            P("pipe", None, "expert"),
            P("pipe", None, "expert"),
            P("pipe", "expert", None),
            P("pipe", "expert", None),
            P("pipe", "expert", None),
            P("pipe", "expert", None),
        ),
        out_specs=(
            P("pipe", "expert", None),
            P("pipe", None, "expert"),
            P("pipe", None, "expert"),
            P("pipe", "expert", None),
            P("pipe", "expert", None),
        ),
        check_vma=False,
    )
```
